256 devices in a mesh: pipe: 16 (over y, x_lo, core), fsdp: 8 (over z), tp: 2 (over x_hi).
Axes of the slice: x: 4 (x_hi: 2, x_lo: 2; x = x_hi * 2 + x_lo), y: 4, z: 8, core: 2. Of those that a mesh axis runs over, the one named last changes fastest.
Arguments:
- act_in: bfloat16 [16, 2, 8, 128, 4096], P('pipe', None, 'fsdp', None, 'tp'), may hold values from -6 to 6
- gate_q: bfloat16 [16, 2, 8, 128, 4096], P('pipe', None, 'fsdp', None, 'tp'), may hold values from -6 to 6
- gate_k: bfloat16 [16, 2, 8, 128, 4096], P('pipe', None, 'fsdp', None, 'tp'), may hold values from -6 to 6
- grad_in: bfloat16 [16, 8, 128, 4096], P('pipe', 'fsdp', None, 'tp'), may hold values from -6 to 6
- weight: bfloat16 [16, 4096, 4096], P('pipe', 'tp', 'fsdp'), may hold values from -0.09375 to 0.09375
- filters: bfloat16 [16, 128, 256], P('pipe', None, 'tp'), may hold values from -0.5 to 0.5
Outputs:
- grad_out: bfloat16 [16, 2, 8, 128, 4096], P('pipe', None, 'fsdp', None, 'tp')
- filter_grad: float32 [16, 128, 256], P('pipe', 'fsdp', 'tp')
The draws below stay inside these ranges and needn't reach their ends.
All inputs are finite; a program needn't handle non-finite values.
Results may differ from the reference program's by a relative error of at most 0.0056.
Values may be sent and summed in bfloat16 or wider, within the bound.
No kernel may reach another device: no remote copies, remote signals or barrier semaphores. Data moves between devices by JAX's collectives and lax.ppermute only.
A program may use at most 128 MiB of HBM per device.

```python
import math
import jax
import jax.numpy as jnp
from jax import lax

D = 4096
TAPS = 128
GROUP = 16
TICKS = 2
LEN = 128
GROUPS = 256
SECTIONS = 16
SEQS = 8


def block_levels(key, shape, pieces, least, largest):
    factor_of, own = 1.0, jax.random.fold_in(key, 6)
    for position, blocks in pieces:
        steps = jnp.exp(jax.random.uniform(jax.random.fold_in(own, position), (blocks,), jnp.float32, least / len(pieces), largest / len(pieces)))
        factor_of = factor_of * jnp.repeat(steps, shape[position] // blocks).reshape([-1 if axis == position else 1 for axis in range(len(shape))])
    return factor_of


def gaussian(stream_key, shape, deviation, limit, pieces=(), kind=jnp.bfloat16):
    values = deviation * jax.random.normal(stream_key, shape, jnp.float32)
    if pieces:
        values = values * block_levels(stream_key, shape, pieces, -0.22, 0.18)
    return jnp.clip(values, -limit, limit).astype(kind)


def setup_inputs(seed: int = 0) -> dict:
    streams_of = jax.random.split(jax.random.key(seed), 7)
    return {
        "act_in": gaussian(streams_of[0], (SECTIONS, TICKS, SEQS, LEN, D), 1.0, 6.0, ((0, 16), (2, 8), (4, 2))),
        "gate_q": gaussian(streams_of[1], (SECTIONS, TICKS, SEQS, LEN, D), 1.0, 6.0, ((0, 16), (2, 8), (4, 2))),
        "gate_k": gaussian(streams_of[2], (SECTIONS, TICKS, SEQS, LEN, D), 1.0, 6.0, ((0, 16), (2, 8), (4, 2))),
        "grad_in": gaussian(streams_of[3], (SECTIONS, SEQS, LEN, D), 1.0, 6.0, ((0, 16), (1, 8), (3, 2))),
        "weight": gaussian(streams_of[4], (SECTIONS, D, D), D ** -0.5, 0.09375, ((0, 16), (1, 2), (2, 8))),
        "filters": gaussian(streams_of[5], (SECTIONS, TAPS, GROUPS), TAPS ** -0.5, 0.5, ((0, 16), (2, 2))),
    }


def section_back(grads, act, gate_one, gate_two, proj, taps_table):
    seqs, seqlen, width = grads.shape
    deriv = jnp.dot(grads.reshape(-1, width), proj.T, preferred_element_type=jnp.float32).reshape(seqs, seqlen, width)
    adj = (gate_one.astype(jnp.float32) * deriv).astype(jnp.bfloat16)
    adj32 = adj.astype(jnp.float32)
    later = jnp.arange(seqlen, dtype=jnp.int32)[None, :] - jnp.arange(seqlen, dtype=jnp.int32)[:, None]
    inside = (later >= 0) & (later < TAPS)
    index = jnp.clip(later, 0, TAPS - 1)
    kernel = jnp.where(inside[:, :, None], taps_table.astype(jnp.float32)[index], jnp.float32(0.0))
    back = jnp.einsum('tug,sugc->stgc', kernel, adj32.reshape(seqs, seqlen, GROUPS, GROUP)).reshape(seqs, seqlen, width)
    result = (grads.astype(jnp.float32) + gate_two.astype(jnp.float32) * back).astype(jnp.bfloat16)
    shaped = (gate_two.astype(jnp.float32) * act.astype(jnp.float32)).astype(jnp.bfloat16)
    padded = jnp.pad(shaped.astype(jnp.float32), ((0, 0), (TAPS, 0), (0, 0)))

    def one_tap(lag):
        moved = lax.dynamic_slice_in_dim(padded, (TAPS - lag).astype(jnp.int32), seqlen, 1)
        return lax.optimization_barrier(jnp.sum((adj32 * moved).reshape(seqs, seqlen, GROUPS, GROUP), axis=(0, 1, 3)))
    filt = lax.map(one_tap, jnp.arange(TAPS, dtype=jnp.int32))
    return (result, filt)

def reference(act_in, gate_q, gate_k, grad_in, weight, filters):
    incoming = grad_in
    outputs = []
    total = jnp.zeros((SECTIONS, TAPS, GROUPS), jnp.float32)
    for tick in range(TICKS):
        if tick > 0:
            incoming = jnp.concatenate([outputs[-1][1:], jnp.zeros_like(outputs[-1][:1])], axis=0)

        def per_section(items):
            return section_back(*items)
        result, filt = lax.map(per_section, (incoming, act_in[:, tick], gate_q[:, tick], gate_k[:, tick], weight, filters))
        outputs.append(result)
        total = total + filt
    scale = 1.0 / math.sqrt(TICKS * SEQS * LEN * GROUP)
    return (jnp.stack(outputs, axis=1), total * scale)
```

```python
import functools
import math

import jax
import jax.numpy as jnp
from jax import lax
from jax.experimental import pallas as pl
from jax.experimental.pallas import tpu as pltpu
from jax.sharding import PartitionSpec as P

BLOCK = 512
VMEM = 40 * 1024 * 1024


def toeplitz_kernel(rows_ref, out_ref):
    groups, seqlen, _ = out_ref.shape
    u = lax.broadcasted_iota(jnp.int32, (seqlen, seqlen), 0)
    t = lax.broadcasted_iota(jnp.int32, (seqlen, seqlen), 1)
    for p in range(groups):
        wide = jnp.broadcast_to(rows_ref[p : p + 1, :], (seqlen, seqlen))
        rolled = pltpu.roll(wide, 1, 1, stride=1, stride_axis=0)
        out_ref[p] = jnp.where(u >= t, rolled, 0.0).astype(jnp.bfloat16)


def toeplitz(rows, step=16):
    groups, seqlen = rows.shape
    return pl.pallas_call(
        toeplitz_kernel,
        grid=(groups // step,),
        in_specs=[pl.BlockSpec((step, seqlen), lambda i: (i, 0))],
        out_specs=pl.BlockSpec((step, seqlen, seqlen), lambda i: (i, 0, 0)),
        out_shape=jax.ShapeDtypeStruct((groups, seqlen, seqlen), jnp.bfloat16),
        name="toeplitz",
    )(rows)


def prepare_kernel(per, act_ref, q_ref, k_ref, qt_ref, kt_ref, late_ref):
    _, seqlen, width = act_ref.shape
    row = lax.broadcasted_iota(jnp.int32, (seqlen, seqlen), 0)
    column = lax.broadcasted_iota(jnp.int32, (seqlen, seqlen), 1)
    flip = jnp.where(row + column == seqlen - 1, 1.0, 0.0).astype(jnp.bfloat16)
    for at in range(0, width, seqlen):
        here = slice(at, at + seqlen)
        qt_ref[here, :] = q_ref[0, :, here].T
        kt_ref[here, :] = k_ref[0, :, here].T
        shaped = (k_ref[0, :, here].astype(jnp.float32) * act_ref[0, :, here].astype(jnp.float32)).astype(jnp.bfloat16)
        late = jnp.dot(flip, shaped, preferred_element_type=jnp.float32).astype(jnp.bfloat16)
        for i in range(seqlen // per):
            late_ref[at // per + i] = late[:, i * per : (i + 1) * per]


def prepare(act, q, k, tick, per):
    _, seqlen, width = act.shape
    groups = width // per
    block = pl.BlockSpec((1, seqlen, width), lambda i: (tick, 0, 0))
    return pl.pallas_call(
        functools.partial(prepare_kernel, per),
        grid=(1,),
        in_specs=[block] * 3,
        out_specs=[whole_spec((width, seqlen))] * 2 + [whole_spec((groups, seqlen, per))],
        out_shape=[jax.ShapeDtypeStruct((width, seqlen), jnp.bfloat16)] * 2
        + [jax.ShapeDtypeStruct((groups, seqlen, per), jnp.bfloat16)],
        compiler_params=pltpu.CompilerParams(vmem_limit_bytes=VMEM),
        name="prepare",
    )(act, q, k)


def correlate(adj, late):
    corr = jnp.dot(late, adj, preferred_element_type=jnp.float32)
    rolled = pltpu.roll(corr, 1, 1, stride=1, stride_axis=0)
    r = lax.broadcasted_iota(jnp.int32, corr.shape, 0)
    lag = lax.broadcasted_iota(jnp.int32, corr.shape, 1)
    return jnp.sum(jnp.where(lag <= r, rolled, 0.0), axis=0, keepdims=True)


def project(offsets, place_ref, g_ref, w_refs, total=None):
    parts, depth, _ = g_ref.shape
    for (offset, first), w_ref in zip(offsets, w_refs):
        g = g_ref[lax.rem(place_ref[0] + (offset + parts), parts), first : first + w_ref.shape[1], :]
        part = jnp.dot(w_ref[...], g, preferred_element_type=jnp.float32)
        total = part if total is None else total + part
    return total


def shape_back(adj, own, k, toe_ref, out_ref, per):
    for p in range(toe_ref.shape[0]):
        at = slice(p * per, (p + 1) * per)
        back = jnp.dot(adj[at], toe_ref[p], preferred_element_type=jnp.float32)
        out_ref[at, :] = (own[at].astype(jnp.float32) + k[at].astype(jnp.float32) * back).astype(jnp.bfloat16)


def partial_kernel(offsets, place_ref, g_ref, *refs):
    count = len(offsets)
    w_refs, out_ref = refs[:count], refs[-1]
    total = refs[count][...] if len(refs) > count + 1 else None
    out_ref[...] = project(offsets, place_ref, g_ref, w_refs, total)


def first_kernel(offsets, per, place_ref, g_ref, *refs):
    count = len(offsets)
    w_refs = refs[:count]
    acc_ref, own_ref, q_ref, k_ref, toe_ref, out_ref, adj_ref = refs[count:]
    deriv = project(offsets, place_ref, g_ref, w_refs, acc_ref[...])
    adj = (q_ref[...].astype(jnp.float32) * deriv).astype(jnp.bfloat16)
    adj_ref[...] = adj
    shape_back(adj, own_ref[...], k_ref[...], toe_ref, out_ref, per)


def last_kernel(offsets, per, place_ref, own_ref, other_ref, *refs):
    count = len(offsets)
    w_refs = refs[:count]
    q_ref, late_ref, term_ref, _, adj_ref, sum_ref, g_ref, lag_ref = refs[count:]
    step = pl.program_id(0)
    parts = own_ref.shape[0]

    @pl.when(step == 0)
    def _():
        g_ref[pl.ds(place_ref[1] * parts, parts)] = own_ref[...]
        g_ref[pl.ds((1 - place_ref[1]) * parts, parts)] = other_ref[...]

    deriv = project(offsets, place_ref, g_ref, w_refs)
    adj = (q_ref[...].astype(jnp.float32) * deriv).astype(jnp.bfloat16)
    adj_ref[...] = adj
    groups = late_ref.shape[0]
    rows = [correlate(adj[p * per : (p + 1) * per], late_ref[p]) for p in range(groups)]
    for p in range(0, groups, 8):
        at = pl.ds(pl.multiple_of(step * groups + p, 8), 8)
        lag_ref[at, :] = term_ref[p : p + 8, :] + jnp.concatenate(rows[p : p + 8], axis=0)

    @pl.when(step == pl.num_programs(0) - 1)
    def _():
        sum_ref[...] = lag_ref[...].T


def lags_kernel(per, adj_ref, late_ref, out_ref):
    for p in range(out_ref.shape[0]):
        out_ref[p : p + 1, :] = correlate(adj_ref[p * per : (p + 1) * per, :], late_ref[p])


def turn_kernel(in_ref, out_ref):
    out_ref[0] = in_ref[...].T


def finish_kernel(per, adj_ref, own_ref, k_ref, toe_ref, held_ref, out_ref, back_ref):
    shape_back(adj_ref[...], own_ref[...], k_ref[...], toe_ref, back_ref, per)
    out_ref[0] = back_ref[...].T


def chan(seqlen):
    return pl.BlockSpec((BLOCK, seqlen), lambda i, *_: (i, 0))


def grouped(tail, per):
    return pl.BlockSpec((BLOCK // per, *tail), lambda i, *_: (i, *([0] * len(tail))))


def whole_spec(shape):
    return pl.BlockSpec(shape, lambda i, *_: (0,) * len(shape))


def call(kernel, place, gs, panels, rest, rest_specs, out_specs, out_shape, name, scratch=()):
    width = panels[0].shape[0]
    size = sum(p.size for p in panels)
    seqlen = gs[0].shape[2]
    return pl.pallas_call(
        kernel,
        grid_spec=pltpu.PrefetchScalarGridSpec(
            num_scalar_prefetch=1,
            grid=(width // BLOCK,),
            in_specs=[whole_spec(g.shape) for g in gs]
            + [pl.BlockSpec((BLOCK, p.shape[1]), lambda i, *_: (i, 0)) for p in panels]
            + rest_specs,
            out_specs=out_specs,
            scratch_shapes=list(scratch),
        ),
        out_shape=out_shape,
        compiler_params=pltpu.CompilerParams(vmem_limit_bytes=VMEM),
        cost_estimate=pl.CostEstimate(flops=2 * size * seqlen, bytes_accessed=2 * size, transcendentals=0),
        name=name,
    )(place, *gs, *panels, *rest)


def partial(place, g, offsets, panels, acc=None):
    seqlen = g.shape[2]
    rest = [] if acc is None else [acc]
    return call(
        functools.partial(partial_kernel, offsets), place, [g], panels, rest, [chan(seqlen)] * len(rest), chan(seqlen),
        jax.ShapeDtypeStruct((panels[0].shape[0], seqlen), jnp.float32), "partial_sums",
    )


def first_part(place, g, offsets, panels, acc, own, q, k, toe, per):
    seqlen = g.shape[2]
    at = chan(seqlen)
    return call(
        functools.partial(first_kernel, offsets, per), place, [g], panels, [acc, own, q, k, toe],
        [at, at, at, at, grouped(toe.shape[1:], per)], [at] * 2,
        [jax.ShapeDtypeStruct(own.shape, jnp.bfloat16)] * 2, "first_tick",
    )


def last_part(place, own, other, offsets, panels, q, late, term, ready, per):
    parts, depth, seqlen = own.shape
    at = chan(seqlen)
    groups = late.shape[0]
    return call(
        functools.partial(last_kernel, offsets, per), place, [own, other], panels, [q, late, term, ready],
        [at, grouped(late.shape[1:], per), grouped((seqlen,), per), pl.BlockSpec(memory_space=pl.ANY)], [at, whole_spec((seqlen, groups))],
        [jax.ShapeDtypeStruct(q.shape, jnp.bfloat16), jax.ShapeDtypeStruct((seqlen, groups), jnp.float32)],
        "last_tick",
        [pltpu.VMEM((2 * parts, depth, seqlen), jnp.bfloat16), pltpu.VMEM((groups, seqlen), jnp.float32)],
    )


def small_cost(width, seqlen):
    return pl.CostEstimate(flops=width * seqlen * seqlen * 8, bytes_accessed=8 * width * seqlen, transcendentals=0)


def lags(adj, late, per):
    width, seqlen = adj.shape
    return pl.pallas_call(
        functools.partial(lags_kernel, per),
        grid=(width // BLOCK,),
        in_specs=[chan(seqlen), grouped(late.shape[1:], per)],
        out_specs=grouped((seqlen,), per),
        out_shape=jax.ShapeDtypeStruct((width // per, seqlen), jnp.float32),
        compiler_params=pltpu.CompilerParams(vmem_limit_bytes=VMEM),
        cost_estimate=small_cost(width, seqlen),
        name="lags",
    )(adj, late)


def turn(value, ticks):
    width, seqlen = value.shape
    return pl.pallas_call(
        turn_kernel,
        grid=(width // BLOCK,),
        in_specs=[chan(seqlen)],
        out_specs=pl.BlockSpec((1, seqlen, BLOCK), lambda i: (0, 0, i)),
        out_shape=jax.ShapeDtypeStruct((ticks, seqlen, width), jnp.bfloat16),
        name="turn",
    )(value)


def finish(adj, own, k, toe, held, tick, per):
    width, seqlen = adj.shape
    return pl.pallas_call(
        functools.partial(finish_kernel, per),
        grid=(width // BLOCK,),
        in_specs=[chan(seqlen)] * 3 + [grouped(toe.shape[1:], per), pl.BlockSpec(memory_space=pl.ANY)],
        out_specs=pl.BlockSpec((1, seqlen, BLOCK), lambda i: (tick, 0, i)),
        out_shape=jax.ShapeDtypeStruct(held.shape, jnp.bfloat16),
        scratch_shapes=[pltpu.VMEM((BLOCK, seqlen), jnp.bfloat16)],
        input_output_aliases={4: 0},
        compiler_params=pltpu.CompilerParams(vmem_limit_bytes=VMEM),
        cost_estimate=small_cost(width, seqlen),
        name="finish",
    )(adj, own, k, toe, held)


def after_kernel(*refs):
    pass


def after(value, *others):
    anywhere = pl.BlockSpec(memory_space=pl.ANY)
    return pl.pallas_call(
        after_kernel,
        in_specs=[anywhere] * (1 + len(others)),
        out_specs=anywhere,
        out_shape=jax.ShapeDtypeStruct(value.shape, value.dtype),
        input_output_aliases={0: 0},
        name="after",
    )(value, *others)


def both_halves(own, other, rank):
    return jnp.concatenate([jnp.where(rank == 0, own, other), jnp.where(rank == 0, other, own)], axis=0)


def round_ring(value, by):
    peers = lax.axis_size("fsdp")
    return lax.ppermute(value, "fsdp", [(i, (i + by) % peers) for i in range(peers)])


def body(act_in, gate_q, gate_k, grad_in, weight, filters):
    ticks, _, seqlen, width = act_in.shape[1:]
    taps, groups = filters.shape[1:]
    per = width // groups
    depth = weight.shape[2]
    sections = lax.axis_size("pipe")
    scale = 1.0 / math.sqrt(ticks * lax.axis_size("fsdp") * seqlen * per)
    rank = lax.axis_index("tp")
    place = jnp.stack([lax.axis_index("fsdp"), rank])
    half = depth // 2
    panels = {(0, first): weight[0, :, first : first + half] for first in (0, half)}

    def circulate(step, first):
        if step < 4 or first == 0:
            panels[-step, first] = round_ring(panels[1 - step, first], 1)
        if step < 4 or first == half:
            panels[step, first] = round_ring(panels[step - 1, first], -1)

    circulate(1, 0)
    circulate(1, half)
    own = grad_in[0, 0].T
    other = lax.ppermute(own, "tp", [(0, 1), (1, 0)])
    acts, qs, ks = act_in[0, :, 0], gate_q[0, :, 0], gate_k[0, :, 0]
    ready = [prepare(acts, qs, ks, i, per) for i in range(ticks)]
    q, k, late = zip(*ready)
    toe = toeplitz(filters[0, ::-1].T.astype(jnp.float32))
    whole = both_halves(own, other, rank).reshape(-1, depth, seqlen)
    circulate(2, 0)
    circulate(2, half)
    panels[2, half] = after(panels[2, half], *ready[0], *ready[1], toe)
    for step in range(3, 5):
        for first in (0, half):
            circulate(step, first)

    def held(*steps):
        return [at for at in sorted(panels) if abs(at[0]) in steps]

    straight = [(s + 1, s) for s in range(sections - 1)]
    crossed = [((s + 1) * 2 + h, s * 2 + 1 - h) for s in range(sections - 1) for h in range(2)]
    acc = None
    for steps in ((0, 1), (2,), (3,)):
        near = held(*steps)
        acc = partial(place, whole, near, [panels[at] for at in near], acc)
    far = held(4)
    out, adj = first_part(place, whole, far, [panels[at] for at in far], acc, own, q[0], k[0], toe, per)
    own = lax.ppermute(out, "pipe", straight)
    other = lax.ppermute(out, ("pipe", "tp"), crossed)
    term = lags(adj, late[0], per)
    grads = turn(out, ticks)
    every = held(0, 1, 2, 3, 4)
    adj, total = last_part(
        place, own.reshape(-1, depth, seqlen), other.reshape(-1, depth, seqlen), every, [panels[at] for at in every],
        q[1], late[1], term, grads, per,
    )
    spread = lax.all_to_all(total.reshape(lax.axis_size("fsdp"), -1, groups), "fsdp", 0, 0, tiled=True)
    grads = finish(adj, own, k[1], toe, grads, 1, per)
    summed = jnp.sum(spread, axis=0) * scale
    return (grads[None, :, None], summed[None])


def solution(mesh):
    placed = (
        P("pipe", None, "fsdp", None, "tp"),
        P("pipe", None, "fsdp", None, "tp"),
        P("pipe", None, "fsdp", None, "tp"),
        P("pipe", "fsdp", None, "tp"),
        P("pipe", "tp", "fsdp"),
        P("pipe", None, "tp"),
    )
    return jax.shard_map(
        body,
        mesh=mesh,
        in_specs=placed,
        out_specs=(P("pipe", None, "fsdp", None, "tp"), P("pipe", "fsdp", "tp")),
        check_vma=False,
    )
```

```python
import functools
import math

import jax
import jax.numpy as jnp
from jax import lax
from jax.experimental import pallas as pl
from jax.experimental.pallas import tpu as pltpu
from jax.sharding import PartitionSpec as P

BLOCK = 512
VMEM = 40 * 1024 * 1024


def toeplitz_kernel(rows_ref, out_ref):
    groups, seqlen, _ = out_ref.shape
    u = lax.broadcasted_iota(jnp.int32, (seqlen, seqlen), 0)
    t = lax.broadcasted_iota(jnp.int32, (seqlen, seqlen), 1)
    for p in range(groups):
        wide = jnp.broadcast_to(rows_ref[p : p + 1, :], (seqlen, seqlen))
        rolled = pltpu.roll(wide, 1, 1, stride=1, stride_axis=0)
        out_ref[p] = jnp.where(u >= t, rolled, 0.0).astype(jnp.bfloat16)


def toeplitz(rows, step=16):
    groups, seqlen = rows.shape
    return pl.pallas_call(
        toeplitz_kernel,
        grid=(groups // step,),
        in_specs=[pl.BlockSpec((step, seqlen), lambda i: (i, 0))],
        out_specs=pl.BlockSpec((step, seqlen, seqlen), lambda i: (i, 0, 0)),
        out_shape=jax.ShapeDtypeStruct((groups, seqlen, seqlen), jnp.bfloat16),
        name="toeplitz",
    )(rows)


def prepare_kernel(act_ref, q_ref, k_ref, qt_ref, kt_ref, late_ref):
    _, seqlen, width = act_ref.shape
    row = lax.broadcasted_iota(jnp.int32, (seqlen, seqlen), 0)
    column = lax.broadcasted_iota(jnp.int32, (seqlen, seqlen), 1)
    flip = jnp.where(row + column == seqlen - 1, 1.0, 0.0).astype(jnp.bfloat16)
    for at in range(0, width, seqlen):
        here = slice(at, at + seqlen)
        qt_ref[here, :] = q_ref[0, :, here].T
        kt_ref[here, :] = k_ref[0, :, here].T
        shaped = (k_ref[0, :, here].astype(jnp.float32) * act_ref[0, :, here].astype(jnp.float32)).astype(jnp.bfloat16)
        late_ref[:, here] = jnp.dot(flip, shaped, preferred_element_type=jnp.float32).astype(jnp.bfloat16)


def prepare(act, q, k, tick):
    _, seqlen, width = act.shape
    block = pl.BlockSpec((1, seqlen, width), lambda i: (tick, 0, 0))
    return pl.pallas_call(
        prepare_kernel,
        grid=(1,),
        in_specs=[block] * 3,
        out_specs=[whole_spec((width, seqlen))] * 2 + [whole_spec((seqlen, width))],
        out_shape=[jax.ShapeDtypeStruct((width, seqlen), jnp.bfloat16)] * 2
        + [jax.ShapeDtypeStruct((seqlen, width), jnp.bfloat16)],
        compiler_params=pltpu.CompilerParams(vmem_limit_bytes=VMEM),
        name="prepare",
    )(act, q, k)


def correlate(adj, late, per):
    width, seqlen = adj.shape
    spread = []
    for at in range(0, width, per):
        above, below = jnp.zeros((at, seqlen), adj.dtype), jnp.zeros((width - at - per, seqlen), adj.dtype)
        spread.append(jnp.concatenate([x for x in (above, adj[at : at + per], below) if x.shape[0]], axis=0))
    corr = jnp.dot(late, jnp.concatenate(spread, axis=1), preferred_element_type=jnp.float32)
    r = lax.broadcasted_iota(jnp.int32, (seqlen, seqlen), 0)
    lag = lax.broadcasted_iota(jnp.int32, (seqlen, seqlen), 1)
    rows = []
    for at in range(0, corr.shape[1], seqlen):
        rolled = pltpu.roll(corr[:, at : at + seqlen], 1, 1, stride=1, stride_axis=0)
        rows.append(jnp.sum(jnp.where(lag <= r, rolled, 0.0), axis=0, keepdims=True))
    return jnp.concatenate(rows, axis=0)


def project(offsets, place_ref, g_ref, w_refs, total=None):
    parts, depth, _ = g_ref.shape
    for (offset, first), w_ref in zip(offsets, w_refs):
        g = g_ref[lax.rem(place_ref[0] + (offset + parts), parts), first : first + w_ref.shape[1], :]
        part = jnp.dot(w_ref[...], g, preferred_element_type=jnp.float32)
        total = part if total is None else total + part
    return total


def shape_back(adj, own, k, toe_ref, out_ref, per):
    for p in range(toe_ref.shape[0]):
        at = slice(p * per, (p + 1) * per)
        back = jnp.dot(adj[at], toe_ref[p], preferred_element_type=jnp.float32)
        out_ref[at, :] = (own[at].astype(jnp.float32) + k[at].astype(jnp.float32) * back).astype(jnp.bfloat16)


def partial_kernel(offsets, place_ref, g_ref, *refs):
    count = len(offsets)
    w_refs, out_ref = refs[:count], refs[-1]
    total = refs[count][...] if len(refs) > count + 1 else None
    out_ref[...] = project(offsets, place_ref, g_ref, w_refs, total)


def first_kernel(offsets, per, place_ref, g_ref, *refs):
    count = len(offsets)
    w_refs = refs[:count]
    acc_ref, own_ref, q_ref, k_ref, toe_ref, out_ref, adj_ref = refs[count:]
    deriv = project(offsets, place_ref, g_ref, w_refs, acc_ref[...])
    adj = (q_ref[...].astype(jnp.float32) * deriv).astype(jnp.bfloat16)
    adj_ref[...] = adj
    shape_back(adj, own_ref[...], k_ref[...], toe_ref, out_ref, per)


def last_kernel(offsets, per, place_ref, own_ref, other_ref, *refs):
    count = len(offsets)
    q_ref, late_ref, term_ref, adj_ref, sum_ref, g_ref, acc_ref, lag_ref, held_ref, sems = refs[count:]
    copies = [pltpu.make_async_copy(refs[i], held_ref.at[i], sems.at[i]) for i in range(count)]
    for copy in copies:
        copy.start()
    parts = own_ref.shape[0]
    g_ref[pl.ds(place_ref[1] * parts, parts)] = own_ref[...]
    g_ref[pl.ds((1 - place_ref[1]) * parts, parts)] = other_ref[...]
    width, seqlen = acc_ref.shape
    peers, depth = g_ref.shape[0], held_ref.shape[2]
    for i, (offset, first) in enumerate(offsets):
        g = g_ref[lax.rem(place_ref[0] + (offset + peers), peers), first : first + depth, :]
        copies[i].wait()
        for row in range(0, width, width // 2):
            at = slice(row, row + width // 2)
            part = jnp.dot(held_ref[i, at, :], g, preferred_element_type=jnp.float32)
            acc_ref[at, :] = part if i == 0 else acc_ref[at, :] + part
    for row in range(0, width, seqlen):
        at = slice(row, row + seqlen)
        adj = (q_ref[at, :].astype(jnp.float32) * acc_ref[at, :]).astype(jnp.bfloat16)
        adj_ref[at, :] = adj
        to = slice(row // per, (row + seqlen) // per)
        lag_ref[to, :] = term_ref[to, :] + correlate(adj, late_ref[:, at], per)
    sum_ref[...] = lag_ref[...].T


def lags_kernel(per, adj_ref, late_ref, out_ref):
    width, seqlen = adj_ref.shape
    for row in range(0, width, seqlen):
        at = slice(row, row + seqlen)
        out_ref[row // per : (row + seqlen) // per, :] = correlate(adj_ref[at, :], late_ref[:, at], per)


def turn_kernel(in_ref, out_ref):
    width, seqlen = in_ref.shape
    for row in range(0, width, seqlen):
        out_ref[0, :, row : row + seqlen] = in_ref[row : row + seqlen, :].T


def finish_kernel(per, adj_ref, own_ref, k_ref, toe_ref, held_ref, out_ref, back_ref):
    shape_back(adj_ref[...], own_ref[...], k_ref[...], toe_ref, back_ref, per)
    width, seqlen = back_ref.shape
    for row in range(0, width, seqlen):
        out_ref[0, :, row : row + seqlen] = back_ref[row : row + seqlen, :].T


def chan(seqlen):
    return pl.BlockSpec((BLOCK, seqlen), lambda i, *_: (i, 0))


def grouped(tail, per):
    return pl.BlockSpec((BLOCK // per, *tail), lambda i, *_: (i, *([0] * len(tail))))


def whole_spec(shape):
    return pl.BlockSpec(shape, lambda i, *_: (0,) * len(shape))


def call(kernel, place, gs, panels, rest, rest_specs, out_specs, out_shape, name, scratch=()):
    width = panels[0].shape[0]
    size = sum(p.size for p in panels)
    seqlen = gs[0].shape[2]
    return pl.pallas_call(
        kernel,
        grid_spec=pltpu.PrefetchScalarGridSpec(
            num_scalar_prefetch=1,
            grid=(width // BLOCK,),
            in_specs=[whole_spec(g.shape) for g in gs]
            + [pl.BlockSpec((BLOCK, p.shape[1]), lambda i, *_: (i, 0)) for p in panels]
            + rest_specs,
            out_specs=out_specs,
            scratch_shapes=list(scratch),
        ),
        out_shape=out_shape,
        compiler_params=pltpu.CompilerParams(vmem_limit_bytes=VMEM),
        cost_estimate=pl.CostEstimate(flops=2 * size * seqlen, bytes_accessed=2 * size, transcendentals=0),
        name=name,
    )(place, *gs, *panels, *rest)


def partial(place, g, offsets, panels, acc=None):
    seqlen = g.shape[2]
    rest = [] if acc is None else [acc]
    return call(
        functools.partial(partial_kernel, offsets), place, [g], panels, rest, [chan(seqlen)] * len(rest), chan(seqlen),
        jax.ShapeDtypeStruct((panels[0].shape[0], seqlen), jnp.float32), "partial_sums",
    )


def first_part(place, g, offsets, panels, acc, own, q, k, toe, per):
    seqlen = g.shape[2]
    at = chan(seqlen)
    return call(
        functools.partial(first_kernel, offsets, per), place, [g], panels, [acc, own, q, k, toe],
        [at, at, at, at, grouped(toe.shape[1:], per)], [at] * 2,
        [jax.ShapeDtypeStruct(own.shape, jnp.bfloat16)] * 2, "first_tick",
    )


def last_part(place, own, other, offsets, panels, q, late, term, per):
    parts, depth, seqlen = own.shape
    width, across = panels[0].shape
    groups = width // per
    size = sum(p.size for p in panels)
    anywhere = pl.BlockSpec(memory_space=pl.ANY)
    return pl.pallas_call(
        functools.partial(last_kernel, offsets, per),
        grid_spec=pltpu.PrefetchScalarGridSpec(
            num_scalar_prefetch=1,
            grid=(1,),
            in_specs=[whole_spec(own.shape)] * 2
            + [anywhere] * len(panels)
            + [whole_spec(q.shape), whole_spec(late.shape), whole_spec(term.shape)],
            out_specs=[whole_spec(q.shape), whole_spec((seqlen, groups))],
            scratch_shapes=[
                pltpu.VMEM((2 * parts, depth, seqlen), jnp.bfloat16),
                pltpu.VMEM((width, seqlen), jnp.float32),
                pltpu.VMEM((groups, seqlen), jnp.float32),
                pltpu.VMEM((len(panels), width, across), jnp.bfloat16),
                pltpu.SemaphoreType.DMA((len(panels),)),
            ],
        ),
        out_shape=[jax.ShapeDtypeStruct(q.shape, jnp.bfloat16), jax.ShapeDtypeStruct((seqlen, groups), jnp.float32)],
        compiler_params=pltpu.CompilerParams(vmem_limit_bytes=VMEM),
        cost_estimate=pl.CostEstimate(flops=2 * size * seqlen, bytes_accessed=2 * size, transcendentals=0),
        name="last_tick",
    )(place, own, other, *panels, q, late, term)


def small_cost(width, seqlen):
    return pl.CostEstimate(flops=width * seqlen * seqlen * 8, bytes_accessed=8 * width * seqlen, transcendentals=0)


def lags(adj, late, per):
    width, seqlen = adj.shape
    return pl.pallas_call(
        functools.partial(lags_kernel, per),
        grid=(width // BLOCK,),
        in_specs=[chan(seqlen), pl.BlockSpec((seqlen, BLOCK), lambda i: (0, i))],
        out_specs=grouped((seqlen,), per),
        out_shape=jax.ShapeDtypeStruct((width // per, seqlen), jnp.float32),
        compiler_params=pltpu.CompilerParams(vmem_limit_bytes=VMEM),
        cost_estimate=small_cost(width, seqlen),
        name="lags",
    )(adj, late)


def turn(value, ticks):
    width, seqlen = value.shape
    return pl.pallas_call(
        turn_kernel,
        grid=(1,),
        in_specs=[whole_spec(value.shape)],
        out_specs=pl.BlockSpec((1, seqlen, width), lambda i: (0, 0, 0)),
        out_shape=jax.ShapeDtypeStruct((ticks, seqlen, width), jnp.bfloat16),
        compiler_params=pltpu.CompilerParams(vmem_limit_bytes=VMEM),
        name="turn",
    )(value)


def finish(adj, own, k, toe, held, tick, per):
    width, seqlen = adj.shape
    return pl.pallas_call(
        functools.partial(finish_kernel, per),
        grid=(width // BLOCK,),
        in_specs=[chan(seqlen)] * 3 + [grouped(toe.shape[1:], per), pl.BlockSpec(memory_space=pl.ANY)],
        out_specs=pl.BlockSpec((1, seqlen, BLOCK), lambda i: (tick, 0, i)),
        out_shape=jax.ShapeDtypeStruct(held.shape, jnp.bfloat16),
        scratch_shapes=[pltpu.VMEM((BLOCK, seqlen), jnp.bfloat16)],
        input_output_aliases={4: 0},
        compiler_params=pltpu.CompilerParams(vmem_limit_bytes=VMEM),
        cost_estimate=small_cost(width, seqlen),
        name="finish",
    )(adj, own, k, toe, held)


def after_kernel(*refs):
    pass


def after(value, *others):
    anywhere = pl.BlockSpec(memory_space=pl.ANY)
    return pl.pallas_call(
        after_kernel,
        in_specs=[anywhere] * (1 + len(others)),
        out_specs=anywhere,
        out_shape=jax.ShapeDtypeStruct(value.shape, value.dtype),
        input_output_aliases={0: 0},
        name="after",
    )(value, *others)


def both_halves(own, other, rank):
    return jnp.concatenate([jnp.where(rank == 0, own, other), jnp.where(rank == 0, other, own)], axis=0)


def round_ring(value, by):
    peers = lax.axis_size("fsdp")
    return lax.ppermute(value, "fsdp", [(i, (i + by) % peers) for i in range(peers)])


def body(act_in, gate_q, gate_k, grad_in, weight, filters):
    ticks, _, seqlen, width = act_in.shape[1:]
    taps, groups = filters.shape[1:]
    per = width // groups
    depth = weight.shape[2]
    sections = lax.axis_size("pipe")
    scale = 1.0 / math.sqrt(ticks * lax.axis_size("fsdp") * seqlen * per)
    rank = lax.axis_index("tp")
    place = jnp.stack([lax.axis_index("fsdp"), rank])
    half = depth // 2
    panels = {(0, first): weight[0, :, first : first + half] for first in (0, half)}

    def circulate(step, first):
        if step < 4 or first == 0:
            panels[-step, first] = round_ring(panels[1 - step, first], 1)
        if step < 4 or first == half:
            panels[step, first] = round_ring(panels[step - 1, first], -1)

    circulate(1, 0)
    circulate(1, half)
    own = grad_in[0, 0].T
    other = lax.ppermute(own, "tp", [(0, 1), (1, 0)])
    acts, qs, ks = act_in[0, :, 0], gate_q[0, :, 0], gate_k[0, :, 0]
    ready = [prepare(acts, qs, ks, i) for i in range(ticks)]
    q, k, late = zip(*ready)
    toe = toeplitz(filters[0, ::-1].T.astype(jnp.float32))
    whole = both_halves(own, other, rank).reshape(-1, depth, seqlen)
    circulate(2, 0)
    circulate(2, half)
    panels[2, half] = after(panels[2, half], *ready[0], *ready[1], toe)
    for step in range(3, 5):
        for first in (0, half):
            circulate(step, first)

    def held(*steps):
        return [at for at in sorted(panels) if abs(at[0]) in steps]

    straight = [(s + 1, s) for s in range(sections - 1)]
    crossed = [((s + 1) * 2 + h, s * 2 + 1 - h) for s in range(sections - 1) for h in range(2)]
    acc = None
    for steps in ((0, 1), (2,), (3,)):
        near = held(*steps)
        acc = partial(place, whole, near, [panels[at] for at in near], acc)
    far = held(4)
    out, adj = first_part(place, whole, far, [panels[at] for at in far], acc, own, q[0], k[0], toe, per)
    own = lax.ppermute(out, "pipe", straight)
    other = lax.ppermute(out, ("pipe", "tp"), crossed)
    term = lags(adj, late[0], per)
    grads = turn(out, ticks)
    every = held(0, 1, 2, 3, 4)
    adj, total = last_part(
        place, own.reshape(-1, depth, seqlen), other.reshape(-1, depth, seqlen), every, [panels[at] for at in every],
        q[1], late[1], term, per,
    )
    spread = lax.all_to_all(total.reshape(lax.axis_size("fsdp"), -1, groups), "fsdp", 0, 0, tiled=True)
    grads = finish(adj, own, k[1], toe, grads, 1, per)
    summed = jnp.sum(spread, axis=0) * scale
    return (grads[None, :, None], summed[None])


def solution(mesh):
    placed = (
        P("pipe", None, "fsdp", None, "tp"),
        P("pipe", None, "fsdp", None, "tp"),
        P("pipe", None, "fsdp", None, "tp"),
        P("pipe", "fsdp", None, "tp"),
        P("pipe", "tp", "fsdp"),
        P("pipe", None, "tp"),
    )
    return jax.shard_map(
        body,
        mesh=mesh,
        in_specs=placed,
        out_specs=(P("pipe", None, "fsdp", None, "tp"), P("pipe", "fsdp", "tp")),
        check_vma=False,
    )
```

```python
import functools
import math

import jax
import jax.numpy as jnp
from jax import lax
from jax.experimental import pallas as pl
from jax.experimental.pallas import tpu as pltpu
from jax.sharding import PartitionSpec as P

BLOCK = 512
VMEM = 40 * 1024 * 1024


def toeplitz_kernel(rows_ref, out_ref):
    groups, seqlen, _ = out_ref.shape
    u = lax.broadcasted_iota(jnp.int32, (seqlen, seqlen), 0)
    t = lax.broadcasted_iota(jnp.int32, (seqlen, seqlen), 1)
    for p in range(groups):
        wide = jnp.broadcast_to(rows_ref[p : p + 1, :], (seqlen, seqlen))
        rolled = pltpu.roll(wide, 1, 1, stride=1, stride_axis=0)
        out_ref[p] = jnp.where(u >= t, rolled, 0.0).astype(jnp.bfloat16)


def toeplitz(rows, step=16):
    groups, seqlen = rows.shape
    return pl.pallas_call(
        toeplitz_kernel,
        grid=(groups // step,),
        in_specs=[pl.BlockSpec((step, seqlen), lambda i: (i, 0))],
        out_specs=pl.BlockSpec((step, seqlen, seqlen), lambda i: (i, 0, 0)),
        out_shape=jax.ShapeDtypeStruct((groups, seqlen, seqlen), jnp.bfloat16),
        name="toeplitz",
    )(rows)


def prepare_kernel(act_ref, q_ref, k_ref, qt_ref, kt_ref, late_ref):
    _, seqlen, width = act_ref.shape
    row = lax.broadcasted_iota(jnp.int32, (seqlen, seqlen), 0)
    column = lax.broadcasted_iota(jnp.int32, (seqlen, seqlen), 1)
    flip = jnp.where(row + column == seqlen - 1, 1.0, 0.0).astype(jnp.bfloat16)
    for at in range(0, width, seqlen):
        here = slice(at, at + seqlen)
        qt_ref[here, :] = q_ref[0, :, here].T
        kt_ref[here, :] = k_ref[0, :, here].T
        shaped = (k_ref[0, :, here].astype(jnp.float32) * act_ref[0, :, here].astype(jnp.float32)).astype(jnp.bfloat16)
        late_ref[:, here] = jnp.dot(flip, shaped, preferred_element_type=jnp.float32).astype(jnp.bfloat16)


def prepare(act, q, k, tick):
    _, seqlen, width = act.shape
    block = pl.BlockSpec((1, seqlen, width), lambda i: (tick, 0, 0))
    return pl.pallas_call(
        prepare_kernel,
        grid=(1,),
        in_specs=[block] * 3,
        out_specs=[whole_spec((width, seqlen))] * 2 + [whole_spec((seqlen, width))],
        out_shape=[jax.ShapeDtypeStruct((width, seqlen), jnp.bfloat16)] * 2
        + [jax.ShapeDtypeStruct((seqlen, width), jnp.bfloat16)],
        compiler_params=pltpu.CompilerParams(vmem_limit_bytes=VMEM),
        name="prepare",
    )(act, q, k)


def correlate(adj, late, per):
    width, seqlen = adj.shape
    spread = []
    for at in range(0, width, per):
        above, below = jnp.zeros((at, seqlen), adj.dtype), jnp.zeros((width - at - per, seqlen), adj.dtype)
        spread.append(jnp.concatenate([x for x in (above, adj[at : at + per], below) if x.shape[0]], axis=0))
    corr = jnp.dot(late, jnp.concatenate(spread, axis=1), preferred_element_type=jnp.float32)
    r = lax.broadcasted_iota(jnp.int32, (seqlen, seqlen), 0)
    lag = lax.broadcasted_iota(jnp.int32, (seqlen, seqlen), 1)
    rows = []
    for at in range(0, corr.shape[1], seqlen):
        rolled = pltpu.roll(corr[:, at : at + seqlen], 1, 1, stride=1, stride_axis=0)
        rows.append(jnp.sum(jnp.where(lag <= r, rolled, 0.0), axis=0, keepdims=True))
    return jnp.concatenate(rows, axis=0)


def project(offsets, place_ref, g_ref, w_refs, total=None):
    parts, depth, _ = g_ref.shape
    for (offset, first), w_ref in zip(offsets, w_refs):
        g = g_ref[lax.rem(place_ref[0] + (offset + parts), parts), first : first + w_ref.shape[1], :]
        part = jnp.dot(w_ref[...], g, preferred_element_type=jnp.float32)
        total = part if total is None else total + part
    return total


def shape_back(adj, own, k, toe_ref, out_ref, per):
    for p in range(toe_ref.shape[0]):
        at = slice(p * per, (p + 1) * per)
        back = jnp.dot(adj[at], toe_ref[p], preferred_element_type=jnp.float32)
        out_ref[at, :] = (own[at].astype(jnp.float32) + k[at].astype(jnp.float32) * back).astype(jnp.bfloat16)


def partial_kernel(offsets, place_ref, g_ref, *refs):
    count = len(offsets)
    w_refs, out_ref = refs[:count], refs[-1]
    total = refs[count][...] if len(refs) > count + 1 else None
    out_ref[...] = project(offsets, place_ref, g_ref, w_refs, total)


def first_kernel(offsets, per, place_ref, g_ref, *refs):
    count = len(offsets)
    w_refs = refs[:count]
    acc_ref, own_ref, q_ref, k_ref, toe_ref, out_ref, adj_ref = refs[count:]
    deriv = project(offsets, place_ref, g_ref, w_refs, acc_ref[...])
    adj = (q_ref[...].astype(jnp.float32) * deriv).astype(jnp.bfloat16)
    adj_ref[...] = adj
    shape_back(adj, own_ref[...], k_ref[...], toe_ref, out_ref, per)


def last_kernel(offsets, per, place_ref, own_ref, other_ref, *refs):
    count = len(offsets)
    q_ref, late_ref, term_ref, _, adj_ref, sum_ref, g_ref, acc_ref, lag_ref, held_ref, sems = refs[count:]
    copies = [pltpu.make_async_copy(refs[i], held_ref.at[i], sems.at[i]) for i in range(count)]
    for copy in copies:
        copy.start()
    parts = own_ref.shape[0]
    g_ref[pl.ds(place_ref[1] * parts, parts)] = own_ref[...]
    g_ref[pl.ds((1 - place_ref[1]) * parts, parts)] = other_ref[...]
    width, seqlen = acc_ref.shape
    peers, depth = g_ref.shape[0], held_ref.shape[2]
    for i, (offset, first) in enumerate(offsets):
        g = g_ref[lax.rem(place_ref[0] + (offset + peers), peers), first : first + depth, :]
        copies[i].wait()
        for row in range(0, width, width // 2):
            at = slice(row, row + width // 2)
            part = jnp.dot(held_ref[i, at, :], g, preferred_element_type=jnp.float32)
            acc_ref[at, :] = part if i == 0 else acc_ref[at, :] + part
    for row in range(0, width, seqlen):
        at = slice(row, row + seqlen)
        adj = (q_ref[at, :].astype(jnp.float32) * acc_ref[at, :]).astype(jnp.bfloat16)
        adj_ref[at, :] = adj
        to = slice(row // per, (row + seqlen) // per)
        lag_ref[to, :] = term_ref[to, :] + correlate(adj, late_ref[:, at], per)
    sum_ref[...] = lag_ref[...].T


def lags_kernel(per, adj_ref, late_ref, out_ref):
    width, seqlen = adj_ref.shape
    for row in range(0, width, seqlen):
        at = slice(row, row + seqlen)
        out_ref[row // per : (row + seqlen) // per, :] = correlate(adj_ref[at, :], late_ref[:, at], per)


def turn_kernel(in_ref, out_ref):
    width, seqlen = in_ref.shape
    for row in range(0, width, seqlen):
        out_ref[0, :, row : row + seqlen] = in_ref[row : row + seqlen, :].T


def finish_kernel(per, adj_ref, own_ref, k_ref, toe_ref, held_ref, out_ref, back_ref):
    shape_back(adj_ref[...], own_ref[...], k_ref[...], toe_ref, back_ref, per)
    width, seqlen = back_ref.shape
    for row in range(0, width, seqlen):
        out_ref[0, :, row : row + seqlen] = back_ref[row : row + seqlen, :].T


def chan(seqlen):
    return pl.BlockSpec((BLOCK, seqlen), lambda i, *_: (i, 0))


def grouped(tail, per):
    return pl.BlockSpec((BLOCK // per, *tail), lambda i, *_: (i, *([0] * len(tail))))


def whole_spec(shape):
    return pl.BlockSpec(shape, lambda i, *_: (0,) * len(shape))


def call(kernel, place, gs, panels, rest, rest_specs, out_specs, out_shape, name, scratch=()):
    width = panels[0].shape[0]
    size = sum(p.size for p in panels)
    seqlen = gs[0].shape[2]
    return pl.pallas_call(
        kernel,
        grid_spec=pltpu.PrefetchScalarGridSpec(
            num_scalar_prefetch=1,
            grid=(width // BLOCK,),
            in_specs=[whole_spec(g.shape) for g in gs]
            + [pl.BlockSpec((BLOCK, p.shape[1]), lambda i, *_: (i, 0)) for p in panels]
            + rest_specs,
            out_specs=out_specs,
            scratch_shapes=list(scratch),
        ),
        out_shape=out_shape,
        compiler_params=pltpu.CompilerParams(vmem_limit_bytes=VMEM),
        cost_estimate=pl.CostEstimate(flops=2 * size * seqlen, bytes_accessed=2 * size, transcendentals=0),
        name=name,
    )(place, *gs, *panels, *rest)


def partial(place, g, offsets, panels, acc=None):
    seqlen = g.shape[2]
    rest = [] if acc is None else [acc]
    return call(
        functools.partial(partial_kernel, offsets), place, [g], panels, rest, [chan(seqlen)] * len(rest), chan(seqlen),
        jax.ShapeDtypeStruct((panels[0].shape[0], seqlen), jnp.float32), "partial_sums",
    )


def first_part(place, g, offsets, panels, acc, own, q, k, toe, per):
    seqlen = g.shape[2]
    at = chan(seqlen)
    return call(
        functools.partial(first_kernel, offsets, per), place, [g], panels, [acc, own, q, k, toe],
        [at, at, at, at, grouped(toe.shape[1:], per)], [at] * 2,
        [jax.ShapeDtypeStruct(own.shape, jnp.bfloat16)] * 2, "first_tick",
    )


def last_part(place, own, other, offsets, panels, q, late, term, ready, per):
    parts, depth, seqlen = own.shape
    width, across = panels[0].shape
    groups = width // per
    size = sum(p.size for p in panels)
    anywhere = pl.BlockSpec(memory_space=pl.ANY)
    return pl.pallas_call(
        functools.partial(last_kernel, offsets, per),
        grid_spec=pltpu.PrefetchScalarGridSpec(
            num_scalar_prefetch=1,
            grid=(1,),
            in_specs=[whole_spec(own.shape)] * 2
            + [anywhere] * len(panels)
            + [whole_spec(q.shape), whole_spec(late.shape), whole_spec(term.shape), anywhere],
            out_specs=[whole_spec(q.shape), whole_spec((seqlen, groups))],
            scratch_shapes=[
                pltpu.VMEM((2 * parts, depth, seqlen), jnp.bfloat16),
                pltpu.VMEM((width, seqlen), jnp.float32),
                pltpu.VMEM((groups, seqlen), jnp.float32),
                pltpu.VMEM((len(panels), width, across), jnp.bfloat16),
                pltpu.SemaphoreType.DMA((len(panels),)),
            ],
        ),
        out_shape=[jax.ShapeDtypeStruct(q.shape, jnp.bfloat16), jax.ShapeDtypeStruct((seqlen, groups), jnp.float32)],
        compiler_params=pltpu.CompilerParams(vmem_limit_bytes=VMEM),
        cost_estimate=pl.CostEstimate(flops=2 * size * seqlen, bytes_accessed=2 * size, transcendentals=0),
        name="last_tick",
    )(place, own, other, *panels, q, late, term, ready)


def small_cost(width, seqlen):
    return pl.CostEstimate(flops=width * seqlen * seqlen * 8, bytes_accessed=8 * width * seqlen, transcendentals=0)


def lags(adj, late, per):
    width, seqlen = adj.shape
    return pl.pallas_call(
        functools.partial(lags_kernel, per),
        grid=(width // BLOCK,),
        in_specs=[chan(seqlen), pl.BlockSpec((seqlen, BLOCK), lambda i: (0, i))],
        out_specs=grouped((seqlen,), per),
        out_shape=jax.ShapeDtypeStruct((width // per, seqlen), jnp.float32),
        compiler_params=pltpu.CompilerParams(vmem_limit_bytes=VMEM),
        cost_estimate=small_cost(width, seqlen),
        name="lags",
    )(adj, late)


def turn(value, ticks):
    width, seqlen = value.shape
    return pl.pallas_call(
        turn_kernel,
        grid=(1,),
        in_specs=[whole_spec(value.shape)],
        out_specs=pl.BlockSpec((1, seqlen, width), lambda i: (0, 0, 0)),
        out_shape=jax.ShapeDtypeStruct((ticks, seqlen, width), jnp.bfloat16),
        compiler_params=pltpu.CompilerParams(vmem_limit_bytes=VMEM),
        name="turn",
    )(value)


def finish(adj, own, k, toe, held, tick, per):
    width, seqlen = adj.shape
    return pl.pallas_call(
        functools.partial(finish_kernel, per),
        grid=(width // BLOCK,),
        in_specs=[chan(seqlen)] * 3 + [grouped(toe.shape[1:], per), pl.BlockSpec(memory_space=pl.ANY)],
        out_specs=pl.BlockSpec((1, seqlen, BLOCK), lambda i: (tick, 0, i)),
        out_shape=jax.ShapeDtypeStruct(held.shape, jnp.bfloat16),
        scratch_shapes=[pltpu.VMEM((BLOCK, seqlen), jnp.bfloat16)],
        input_output_aliases={4: 0},
        compiler_params=pltpu.CompilerParams(vmem_limit_bytes=VMEM),
        cost_estimate=small_cost(width, seqlen),
        name="finish",
    )(adj, own, k, toe, held)


def after_kernel(*refs):
    pass


def after(value, *others):
    anywhere = pl.BlockSpec(memory_space=pl.ANY)
    return pl.pallas_call(
        after_kernel,
        in_specs=[anywhere] * (1 + len(others)),
        out_specs=anywhere,
        out_shape=jax.ShapeDtypeStruct(value.shape, value.dtype),
        input_output_aliases={0: 0},
        name="after",
    )(value, *others)


def both_halves(own, other, rank):
    return jnp.concatenate([jnp.where(rank == 0, own, other), jnp.where(rank == 0, other, own)], axis=0)


def round_ring(value, by):
    peers = lax.axis_size("fsdp")
    return lax.ppermute(value, "fsdp", [(i, (i + by) % peers) for i in range(peers)])


def body(act_in, gate_q, gate_k, grad_in, weight, filters):
    ticks, _, seqlen, width = act_in.shape[1:]
    taps, groups = filters.shape[1:]
    per = width // groups
    depth = weight.shape[2]
    sections = lax.axis_size("pipe")
    scale = 1.0 / math.sqrt(ticks * lax.axis_size("fsdp") * seqlen * per)
    rank = lax.axis_index("tp")
    place = jnp.stack([lax.axis_index("fsdp"), rank])
    half = depth // 2
    panels = {(0, first): weight[0, :, first : first + half] for first in (0, half)}

    def circulate(step, first):
        if step < 4 or first == 0:
            panels[-step, first] = round_ring(panels[1 - step, first], 1)
        if step < 4 or first == half:
            panels[step, first] = round_ring(panels[step - 1, first], -1)

    circulate(1, 0)
    circulate(1, half)
    own = grad_in[0, 0].T
    other = lax.ppermute(own, "tp", [(0, 1), (1, 0)])
    acts, qs, ks = act_in[0, :, 0], gate_q[0, :, 0], gate_k[0, :, 0]
    ready = [prepare(acts, qs, ks, i) for i in range(ticks)]
    q, k, late = zip(*ready)
    toe = toeplitz(filters[0, ::-1].T.astype(jnp.float32))
    whole = both_halves(own, other, rank).reshape(-1, depth, seqlen)
    panels[1, half] = after(panels[1, half], *ready[0], *ready[1], toe)
    circulate(2, 0)
    circulate(2, half)
    for step in range(3, 5):
        for first in (0, half):
            circulate(step, first)

    def held(*steps):
        return [at for at in sorted(panels) if abs(at[0]) in steps]

    straight = [(s + 1, s) for s in range(sections - 1)]
    crossed = [((s + 1) * 2 + h, s * 2 + 1 - h) for s in range(sections - 1) for h in range(2)]
    acc = None
    for steps in ((0, 1), (2,), (3,)):
        near = held(*steps)
        acc = partial(place, whole, near, [panels[at] for at in near], acc)
    far = held(4)
    out, adj = first_part(place, whole, far, [panels[at] for at in far], acc, own, q[0], k[0], toe, per)
    own = lax.ppermute(out, "pipe", straight)
    other = lax.ppermute(out, ("pipe", "tp"), crossed)
    term = lags(adj, late[0], per)
    grads = turn(out, ticks)
    every = held(0, 1, 2, 3, 4)
    adj, total = last_part(
        place, own.reshape(-1, depth, seqlen), other.reshape(-1, depth, seqlen), every, [panels[at] for at in every],
        q[1], late[1], term, grads, per,
    )
    spread = lax.all_to_all(total.reshape(lax.axis_size("fsdp"), -1, groups), "fsdp", 0, 0, tiled=True)
    grads = finish(adj, own, k[1], toe, grads, 1, per)
    summed = jnp.sum(spread, axis=0) * scale
    return (grads[None, :, None], summed[None])


def solution(mesh):
    placed = (
        P("pipe", None, "fsdp", None, "tp"),
        P("pipe", None, "fsdp", None, "tp"),
        P("pipe", None, "fsdp", None, "tp"),
        P("pipe", "fsdp", None, "tp"),
        P("pipe", "tp", "fsdp"),
        P("pipe", None, "tp"),
    )
    return jax.shard_map(
        body,
        mesh=mesh,
        in_specs=placed,
        out_specs=(P("pipe", None, "fsdp", None, "tp"), P("pipe", "fsdp", "tp")),
        check_vma=False,
    )
```

```python
import functools
import math

import jax
import jax.numpy as jnp
from jax import lax
from jax.experimental import pallas as pl
from jax.experimental.pallas import tpu as pltpu
from jax.sharding import PartitionSpec as P

BLOCK = 512
VMEM = 40 * 1024 * 1024


def toeplitz_kernel(rows_ref, out_ref):
    groups, seqlen, _ = out_ref.shape
    u = lax.broadcasted_iota(jnp.int32, (seqlen, seqlen), 0)
    t = lax.broadcasted_iota(jnp.int32, (seqlen, seqlen), 1)
    for p in range(groups):
        wide = jnp.broadcast_to(rows_ref[p : p + 1, :], (seqlen, seqlen))
        rolled = pltpu.roll(wide, 1, 1, stride=1, stride_axis=0)
        out_ref[p] = jnp.where(u >= t, rolled, 0.0).astype(jnp.bfloat16)


def toeplitz(rows, step=16):
    groups, seqlen = rows.shape
    return pl.pallas_call(
        toeplitz_kernel,
        grid=(groups // step,),
        in_specs=[pl.BlockSpec((step, seqlen), lambda i: (i, 0))],
        out_specs=pl.BlockSpec((step, seqlen, seqlen), lambda i: (i, 0, 0)),
        out_shape=jax.ShapeDtypeStruct((groups, seqlen, seqlen), jnp.bfloat16),
        name="toeplitz",
    )(rows)


def prepare_kernel(act_ref, q_ref, k_ref, qt_ref, kt_ref, late_ref):
    _, seqlen, width = act_ref.shape
    row = lax.broadcasted_iota(jnp.int32, (seqlen, seqlen), 0)
    column = lax.broadcasted_iota(jnp.int32, (seqlen, seqlen), 1)
    flip = jnp.where(row + column == seqlen - 1, 1.0, 0.0).astype(jnp.bfloat16)
    for at in range(0, width, seqlen):
        here = slice(at, at + seqlen)
        qt_ref[here, :] = q_ref[0, :, here].T
        kt_ref[here, :] = k_ref[0, :, here].T
        shaped = (k_ref[0, :, here].astype(jnp.float32) * act_ref[0, :, here].astype(jnp.float32)).astype(jnp.bfloat16)
        late_ref[:, here] = jnp.dot(flip, shaped, preferred_element_type=jnp.float32).astype(jnp.bfloat16)


def prepare(act, q, k, tick):
    _, seqlen, width = act.shape
    block = pl.BlockSpec((1, seqlen, width), lambda i: (tick, 0, 0))
    return pl.pallas_call(
        prepare_kernel,
        grid=(1,),
        in_specs=[block] * 3,
        out_specs=[whole_spec((width, seqlen))] * 2 + [whole_spec((seqlen, width))],
        out_shape=[jax.ShapeDtypeStruct((width, seqlen), jnp.bfloat16)] * 2
        + [jax.ShapeDtypeStruct((seqlen, width), jnp.bfloat16)],
        compiler_params=pltpu.CompilerParams(vmem_limit_bytes=VMEM),
        name="prepare",
    )(act, q, k)


def correlate(adj, late, per):
    width, seqlen = adj.shape
    spread = []
    for at in range(0, width, per):
        above, below = jnp.zeros((at, seqlen), adj.dtype), jnp.zeros((width - at - per, seqlen), adj.dtype)
        spread.append(jnp.concatenate([x for x in (above, adj[at : at + per], below) if x.shape[0]], axis=0))
    corr = jnp.dot(late, jnp.concatenate(spread, axis=1), preferred_element_type=jnp.float32)
    r = lax.broadcasted_iota(jnp.int32, (seqlen, seqlen), 0)
    lag = lax.broadcasted_iota(jnp.int32, (seqlen, seqlen), 1)
    rows = []
    for at in range(0, corr.shape[1], seqlen):
        rolled = pltpu.roll(corr[:, at : at + seqlen], 1, 1, stride=1, stride_axis=0)
        rows.append(jnp.sum(jnp.where(lag <= r, rolled, 0.0), axis=0, keepdims=True))
    return jnp.concatenate(rows, axis=0)


def project(offsets, place_ref, g_ref, w_refs, total=None):
    parts, depth, _ = g_ref.shape
    for (offset, first), w_ref in zip(offsets, w_refs):
        g = g_ref[lax.rem(place_ref[0] + (offset + parts), parts), first : first + w_ref.shape[1], :]
        part = jnp.dot(w_ref[...], g, preferred_element_type=jnp.float32)
        total = part if total is None else total + part
    return total


def shape_back(adj, own, k, toe_ref, out_ref, per):
    for p in range(toe_ref.shape[0]):
        at = slice(p * per, (p + 1) * per)
        back = jnp.dot(adj[at], toe_ref[p], preferred_element_type=jnp.float32)
        out_ref[at, :] = (own[at].astype(jnp.float32) + k[at].astype(jnp.float32) * back).astype(jnp.bfloat16)


def partial_kernel(offsets, place_ref, g_ref, *refs):
    count = len(offsets)
    w_refs, out_ref = refs[:count], refs[-1]
    total = refs[count][...] if len(refs) > count + 1 else None
    out_ref[...] = project(offsets, place_ref, g_ref, w_refs, total)


def first_kernel(offsets, per, place_ref, g_ref, *refs):
    count = len(offsets)
    w_refs = refs[:count]
    acc_ref, own_ref, q_ref, k_ref, toe_ref, out_ref, adj_ref = refs[count:]
    deriv = project(offsets, place_ref, g_ref, w_refs, acc_ref[...])
    adj = (q_ref[...].astype(jnp.float32) * deriv).astype(jnp.bfloat16)
    adj_ref[...] = adj
    shape_back(adj, own_ref[...], k_ref[...], toe_ref, out_ref, per)


def second_kernel(offsets, per, place_ref, g_ref, *refs):
    *given, _, out_ref, adj_ref = refs
    first_kernel(offsets, per, place_ref, g_ref, *given, out_ref, adj_ref)


def last_kernel(offsets, pieces, per, place_ref, own_lo, own_hi, other_lo, other_hi, *refs):
    q_ref, late_ref, term_ref, adj_ref, sum_ref, g_ref, acc_ref, lag_ref, held_ref, sems = refs[len(pieces) :]
    copies = [
        pltpu.make_async_copy(refs[n], held_ref.at[i, row : row + rows, :], sems.at[n])
        for n, (i, row, rows) in enumerate(pieces)
    ]
    for copy in copies:
        copy.start()
    parts = own_lo.shape[0]
    for side, lo, hi in ((place_ref[1], own_lo, own_hi), (1 - place_ref[1], other_lo, other_hi)):
        g_ref[pl.ds(side * 2 * parts, parts)] = lo[...]
        g_ref[pl.ds(side * 2 * parts + parts, parts)] = hi[...]
    width, seqlen = acc_ref.shape
    peers, depth = g_ref.shape[0], held_ref.shape[2]
    for i, (offset, first) in enumerate(offsets):
        g = g_ref[lax.rem(place_ref[0] + (offset + peers), peers), first : first + depth, :]
        for copy, piece in zip(copies, pieces):
            if piece[0] == i:
                copy.wait()
        for row in range(0, width, width // 2):
            at = slice(row, row + width // 2)
            part = jnp.dot(held_ref[i, at, :], g, preferred_element_type=jnp.float32)
            acc_ref[at, :] = part if i == 0 else acc_ref[at, :] + part
    for row in range(0, width, seqlen):
        at = slice(row, row + seqlen)
        adj = (q_ref[at, :].astype(jnp.float32) * acc_ref[at, :]).astype(jnp.bfloat16)
        adj_ref[at, :] = adj
        to = slice(row // per, (row + seqlen) // per)
        lag_ref[to, :] = term_ref[to, :] + correlate(adj, late_ref[:, at], per)
    sum_ref[...] = lag_ref[...].T


def lags_kernel(per, adj_lo, adj_hi, late_ref, out_ref):
    width, seqlen = adj_lo.shape
    adj = jnp.where(pl.program_id(0) < pl.num_programs(0) // 2, adj_lo[...], adj_hi[...])
    for row in range(0, width, seqlen):
        at = slice(row, row + seqlen)
        out_ref[row // per : (row + seqlen) // per, :] = correlate(adj[at, :], late_ref[:, at], per)


def turn_kernel(lo_ref, hi_ref, out_ref):
    width, seqlen = lo_ref.shape
    for side, ref in enumerate((lo_ref, hi_ref)):
        for row in range(0, width, seqlen):
            to = side * width + row
            out_ref[0, :, to : to + seqlen] = ref[row : row + seqlen, :].T


def finish_kernel(per, adj_ref, own_lo, own_hi, k_ref, toe_ref, held_ref, out_ref, back_ref):
    own = jnp.where(pl.program_id(0) < pl.num_programs(0) // 2, own_lo[...], own_hi[...])
    shape_back(adj_ref[...], own, k_ref[...], toe_ref, back_ref, per)
    width, seqlen = back_ref.shape
    for row in range(0, width, seqlen):
        out_ref[0, :, row : row + seqlen] = back_ref[row : row + seqlen, :].T


def chan(seqlen):
    return pl.BlockSpec((BLOCK, seqlen), lambda i, *_: (i, 0))


def grouped(tail, per):
    return pl.BlockSpec((BLOCK // per, *tail), lambda i, *_: (i, *([0] * len(tail))))


def whole_spec(shape):
    return pl.BlockSpec(shape, lambda i, *_: (0,) * len(shape))


def call(kernel, place, gs, panels, rest, rest_specs, out_specs, out_shape, name, scratch=()):
    width = panels[0].shape[0]
    size = sum(p.size for p in panels)
    seqlen = gs[0].shape[2]
    return pl.pallas_call(
        kernel,
        grid_spec=pltpu.PrefetchScalarGridSpec(
            num_scalar_prefetch=1,
            grid=(width // BLOCK,),
            in_specs=[whole_spec(g.shape) for g in gs]
            + [pl.BlockSpec((BLOCK, p.shape[1]), lambda i, *_: (i, 0)) for p in panels]
            + rest_specs,
            out_specs=out_specs,
            scratch_shapes=list(scratch),
        ),
        out_shape=out_shape,
        compiler_params=pltpu.CompilerParams(vmem_limit_bytes=VMEM),
        cost_estimate=pl.CostEstimate(flops=2 * size * seqlen, bytes_accessed=2 * size, transcendentals=0),
        name=name,
    )(place, *gs, *panels, *rest)


def partial(place, g, offsets, panels, acc=None):
    seqlen = g.shape[2]
    rest = [] if acc is None else [acc]
    return call(
        functools.partial(partial_kernel, offsets), place, [g], panels, rest, [chan(seqlen)] * len(rest), chan(seqlen),
        jax.ShapeDtypeStruct((panels[0].shape[0], seqlen), jnp.float32), "partial_sums",
    )


def first_part(place, g, offsets, panels, acc, own, q, k, toe, arrived, per):
    seqlen = g.shape[2]
    width = own.shape[0]
    half = width // 2 // BLOCK
    skip = half if arrived else 0
    piece = jax.ShapeDtypeStruct((width // 2, seqlen), jnp.bfloat16)
    size = sum(p.size for p in panels)
    return pl.pallas_call(
        functools.partial(second_kernel if arrived else first_kernel, offsets, per),
        grid_spec=pltpu.PrefetchScalarGridSpec(
            num_scalar_prefetch=1,
            grid=(half,),
            in_specs=[whole_spec(g.shape)]
            + [pl.BlockSpec((BLOCK, p.shape[1]), lambda i, *_: (i, 0)) for p in panels]
            + [pl.BlockSpec((BLOCK, seqlen), lambda i, *_: (i + skip, 0))] * 4
            + [pl.BlockSpec((BLOCK // per, *toe.shape[1:]), lambda i, *_: (i + skip, 0, 0))]
            + [pl.BlockSpec(memory_space=pl.ANY)] * len(arrived),
            out_specs=[chan(seqlen)] * 2,
        ),
        out_shape=[piece] * 2,
        compiler_params=pltpu.CompilerParams(vmem_limit_bytes=VMEM),
        cost_estimate=pl.CostEstimate(flops=2 * size * seqlen, bytes_accessed=2 * size, transcendentals=0),
        name="first_tick_upper" if arrived else "first_tick_lower",
    )(place, g, *panels, acc, own, q, k, toe, *arrived)


def last_part(place, sides, offsets, panels, q, late, term, per):
    parts, depth, seqlen = sides[0].shape
    width = q.shape[0]
    groups = width // per
    flat, pieces = [], []
    for i, panel in enumerate(panels):
        row = 0
        for piece in panel:
            flat.append(piece)
            pieces.append((i, row, piece.shape[0]))
            row += piece.shape[0]
    across = flat[0].shape[1]
    size = sum(p.size for p in flat)
    return pl.pallas_call(
        functools.partial(last_kernel, offsets, tuple(pieces), per),
        grid_spec=pltpu.PrefetchScalarGridSpec(
            num_scalar_prefetch=1,
            grid=(1,),
            in_specs=[whole_spec(side.shape) for side in sides]
            + [pl.BlockSpec(memory_space=pl.ANY)] * len(flat)
            + [whole_spec(q.shape), whole_spec(late.shape), whole_spec(term.shape)],
            out_specs=[whole_spec(q.shape), whole_spec((seqlen, groups))],
            scratch_shapes=[
                pltpu.VMEM((4 * parts, depth, seqlen), jnp.bfloat16),
                pltpu.VMEM((width, seqlen), jnp.float32),
                pltpu.VMEM((groups, seqlen), jnp.float32),
                pltpu.VMEM((len(panels), width, across), jnp.bfloat16),
                pltpu.SemaphoreType.DMA((len(flat),)),
            ],
        ),
        out_shape=[jax.ShapeDtypeStruct(q.shape, jnp.bfloat16), jax.ShapeDtypeStruct((seqlen, groups), jnp.float32)],
        compiler_params=pltpu.CompilerParams(vmem_limit_bytes=VMEM),
        cost_estimate=pl.CostEstimate(flops=2 * size * seqlen, bytes_accessed=2 * size, transcendentals=0),
        name="last_tick",
    )(place, *sides, *flat, q, late, term)


def small_cost(width, seqlen):
    return pl.CostEstimate(flops=width * seqlen * seqlen * 8, bytes_accessed=8 * width * seqlen, transcendentals=0)


def lags(adj_lo, adj_hi, late, per):
    seqlen, width = late.shape
    half = width // 2 // BLOCK
    return pl.pallas_call(
        functools.partial(lags_kernel, per),
        grid=(width // BLOCK,),
        in_specs=[
            pl.BlockSpec((BLOCK, seqlen), lambda i: (jnp.minimum(i, half - 1), 0)),
            pl.BlockSpec((BLOCK, seqlen), lambda i: (jnp.maximum(i - half, 0), 0)),
            pl.BlockSpec((seqlen, BLOCK), lambda i: (0, i)),
        ],
        out_specs=pl.BlockSpec((BLOCK // per, seqlen), lambda i: (i, 0)),
        out_shape=jax.ShapeDtypeStruct((width // per, seqlen), jnp.float32),
        compiler_params=pltpu.CompilerParams(vmem_limit_bytes=VMEM),
        cost_estimate=small_cost(width, seqlen),
        name="lags",
    )(adj_lo, adj_hi, late)


def turn(lo, hi, ticks):
    rows, seqlen = lo.shape
    return pl.pallas_call(
        turn_kernel,
        grid=(1,),
        in_specs=[whole_spec(lo.shape)] * 2,
        out_specs=pl.BlockSpec((1, seqlen, 2 * rows), lambda i: (0, 0, 0)),
        out_shape=jax.ShapeDtypeStruct((ticks, seqlen, 2 * rows), jnp.bfloat16),
        compiler_params=pltpu.CompilerParams(vmem_limit_bytes=VMEM),
        name="turn",
    )(lo, hi)


def finish(adj, own_lo, own_hi, k, toe, held, tick, per):
    width, seqlen = adj.shape
    half = width // 2 // BLOCK
    below = pl.BlockSpec((BLOCK, seqlen), lambda i: (jnp.minimum(i, half - 1), 0))
    above = pl.BlockSpec((BLOCK, seqlen), lambda i: (jnp.maximum(i - half, 0), 0))
    return pl.pallas_call(
        functools.partial(finish_kernel, per),
        grid=(width // BLOCK,),
        in_specs=[chan(seqlen), below, above, chan(seqlen)] + [grouped(toe.shape[1:], per), pl.BlockSpec(memory_space=pl.ANY)],
        out_specs=pl.BlockSpec((1, seqlen, BLOCK), lambda i: (tick, 0, i)),
        out_shape=jax.ShapeDtypeStruct(held.shape, jnp.bfloat16),
        scratch_shapes=[pltpu.VMEM((BLOCK, seqlen), jnp.bfloat16)],
        input_output_aliases={5: 0},
        compiler_params=pltpu.CompilerParams(vmem_limit_bytes=VMEM),
        cost_estimate=small_cost(width, seqlen),
        name="finish",
    )(adj, own_lo, own_hi, k, toe, held)


def after_kernel(*refs):
    pass


def after(value, *others):
    anywhere = pl.BlockSpec(memory_space=pl.ANY)
    return pl.pallas_call(
        after_kernel,
        in_specs=[anywhere] * (1 + len(others)),
        out_specs=anywhere,
        out_shape=jax.ShapeDtypeStruct(value.shape, value.dtype),
        input_output_aliases={0: 0},
        name="after",
    )(value, *others)


def both_halves(own, other, rank):
    return jnp.concatenate([jnp.where(rank == 0, own, other), jnp.where(rank == 0, other, own)], axis=0)


def round_ring(value, by):
    peers = lax.axis_size("fsdp")
    return lax.ppermute(value, "fsdp", [(i, (i + by) % peers) for i in range(peers)])


def body(act_in, gate_q, gate_k, grad_in, weight, filters):
    ticks, _, seqlen, width = act_in.shape[1:]
    taps, groups = filters.shape[1:]
    per = width // groups
    depth = weight.shape[2]
    sections = lax.axis_size("pipe")
    scale = 1.0 / math.sqrt(ticks * lax.axis_size("fsdp") * seqlen * per)
    rank = lax.axis_index("tp")
    place = jnp.stack([lax.axis_index("fsdp"), rank])
    half = depth // 2
    panels = {(0, first): weight[0, :, first : first + half] for first in (0, half)}

    def circulate(step, first):
        panels[-step, first] = round_ring(panels[1 - step, first], 1)
        panels[step, first] = round_ring(panels[step - 1, first], -1)

    circulate(1, 0)
    circulate(1, half)
    own = grad_in[0, 0].T
    other = lax.ppermute(own, "tp", [(0, 1), (1, 0)])
    acts, qs, ks = act_in[0, :, 0], gate_q[0, :, 0], gate_k[0, :, 0]
    ready = [prepare(acts, qs, ks, i) for i in range(ticks)]
    q, k, late = zip(*ready)
    toe = toeplitz(filters[0, ::-1].T.astype(jnp.float32))
    whole = both_halves(own, other, rank).reshape(-1, depth, seqlen)
    panels[1, half] = after(panels[1, half], *ready[0], *ready[1], toe)
    circulate(2, 0)
    circulate(2, half)
    for first in (0, half):
        circulate(3, first)
    def held(*steps):
        return [at for at in sorted(panels) if abs(at[0]) in steps]

    straight = [(s + 1, s) for s in range(sections - 1)]
    crossed = [((s + 1) * 2 + h, s * 2 + 1 - h) for s in range(sections - 1) for h in range(2)]
    acc = None
    for steps in ((0, 1), (2,)):
        near = held(*steps)
        acc = partial(place, whole, near, [panels[at] for at in near], acc)
    rows = width // 2
    far = {}
    for by, first in ((1, 0), (-1, half)):
        source = panels[by * -3, first]
        far[by * -4, first] = [round_ring(source[:rows], by), round_ring(after(source[rows:], acc), by)]
    near = held(3)
    acc = partial(place, whole, near, [panels[at] for at in near], acc)
    ends = sorted(far)
    out_lo, adj_lo = first_part(
        place, whole, ends, [far[at][0] for at in ends], acc, own, q[0], k[0], toe, (), per
    )
    other_lo = lax.ppermute(out_lo, ("pipe", "tp"), crossed)
    own_lo = lax.ppermute(out_lo, "pipe", straight)
    out_hi, adj_hi = first_part(
        place, whole, ends, [far[at][1] for at in ends], acc, own, q[0], k[0], toe, (other_lo,), per
    )
    other_hi = lax.ppermute(out_hi, ("pipe", "tp"), crossed)
    own_hi = lax.ppermute(out_hi, "pipe", straight)
    term = lags(adj_lo, adj_hi, late[0], per)
    grads = turn(out_lo, out_hi, ticks)
    near = held(0, 1, 2, 3)
    adj, total = last_part(
        place, [x.reshape(-1, depth, seqlen) for x in (own_lo, own_hi, other_lo, other_hi)],
        near + ends, [[panels[at]] for at in near] + [far[at] for at in ends], q[1], late[1], term, per,
    )
    spread = lax.all_to_all(total.reshape(lax.axis_size("fsdp"), -1, groups), "fsdp", 0, 0, tiled=True)
    grads = finish(adj, own_lo, own_hi, k[1], toe, grads, 1, per)
    summed = jnp.sum(spread, axis=0) * scale
    return (grads[None, :, None], summed[None])


def solution(mesh):
    placed = (
        P("pipe", None, "fsdp", None, "tp"),
        P("pipe", None, "fsdp", None, "tp"),
        P("pipe", None, "fsdp", None, "tp"),
        P("pipe", "fsdp", None, "tp"),
        P("pipe", "tp", "fsdp"),
        P("pipe", None, "tp"),
    )
    return jax.shard_map(
        body,
        mesh=mesh,
        in_specs=placed,
        out_specs=(P("pipe", None, "fsdp", None, "tp"), P("pipe", "fsdp", "tp")),
        check_vma=False,
    )
```
